32 devices in a mesh: row: 4 (over y, x), col: 8 (over z, core).
Axes of the slice: x: 2, y: 2, z: 4, core: 2. Of those that a mesh axis runs over, the one named last changes fastest.
Arguments:
- tokens: bfloat16 [64, 12288], P('col', 'row'), may hold values from -6 to 6
- cotangent: bfloat16 [64, 12288], P('col', 'row'), may hold values from -3 to 3
- weight_in: bfloat16 [12288, 24576], P('row', 'col'), may hold values from -0.0546875 to 0.0546875
- weight_out: bfloat16 [24576, 12288], P('col', 'row'), may hold values from -0.0390625 to 0.0390625
Outputs:
- mixed: bfloat16 [64, 12288], P('col', 'row')
- grad_tokens: bfloat16 [64, 12288], P('col', 'row')
- grad_in: bfloat16 [12288, 24576], P('row', 'col')
- grad_out: bfloat16 [24576, 12288], P('col', 'row')
The draws below stay inside these ranges and needn't reach their ends.
All inputs are finite; a program needn't handle non-finite values.
Results may differ from the reference program's by a relative error of at most 0.0049.
Values may be sent and summed in bfloat16 or wider, within the bound.
No kernel may reach another device: no remote copies, remote signals or barrier semaphores. Data moves between devices by JAX's collectives and lax.ppermute only.
A program may use at most 128 MiB of HBM per device.

```python
import jax
import jax.numpy as jnp
from jax import lax

D = 12288
FF = 24576
TOKENS = 64


def shard_levels(key, shape, split, smallest, top_value):
    def one(position, blocks):
        steps = jax.random.uniform(jax.random.fold_in(jax.random.fold_in(key, 6), position), (blocks,), jnp.float32, smallest / len(split), top_value / len(split))
        return jnp.repeat(jnp.exp(steps), shape[position] // blocks).reshape((-1,) + (1,) * (len(shape) - position - 1))

    loudness = one(*split[0])
    for cut in split[1:]:
        loudness = loudness * one(*cut)
    return loudness


def gaussian(stream_key, dims, deviation, bound, split=(), held_as=jnp.bfloat16):
    values = jax.random.normal(stream_key, dims, jnp.float32) * deviation
    if len(split) > 0:
        values = shard_levels(stream_key, dims, split, -0.22, 0.18) * values
    return jnp.clip(values, min=-bound, max=bound).astype(held_as)


def setup_inputs(seed: int = 0) -> dict:
    key_list = jax.random.split(jax.random.key(seed), 5)
    tokens = gaussian(key_list[0], (TOKENS, D), 1.0, 6.0, ((0, 8), (1, 4)))
    cotangent = gaussian(key_list[1], (TOKENS, D), 0.5, 3.0, ((0, 8), (1, 4)))
    weight_in = gaussian(key_list[2], (D, FF), D ** -0.5, 0.0546875, ((0, 4), (1, 8)))
    weight_out = gaussian(key_list[3], (FF, D), FF ** -0.5, 0.0390625, ((0, 8), (1, 4)))
    return {"tokens": tokens, "cotangent": cotangent, "weight_in": weight_in, "weight_out": weight_out}


def gelu_parts(pre_act):
    normal_cdf = 0.5 * (1.0 + jax.scipy.special.erf(pre_act * 0.7071067811865476))
    density = jnp.exp(-0.5 * pre_act * pre_act) * 0.3989422804014327
    return pre_act * normal_cdf, normal_cdf + pre_act * density


def contract_first(left_side, right_side):
    return lax.dot_general(left_side, right_side, (((0,), (0,)), ((), ())), preferred_element_type=jnp.float32)


def contract_last(left_side, right_side):
    return lax.dot_general(left_side, right_side, (((1,), (1,)), ((), ())), preferred_element_type=jnp.float32)


def reference(tokens, cotangent, weight_in, weight_out):
    pre_act = jnp.dot(tokens, weight_in, preferred_element_type=jnp.float32)
    gelu_value, gelu_slope = gelu_parts(pre_act)
    hidden = gelu_value.astype(jnp.bfloat16)
    mixed = jnp.dot(hidden, weight_out, preferred_element_type=jnp.float32).astype(jnp.bfloat16)
    grad_hidden = contract_last(cotangent, weight_out)
    grad_pre = (grad_hidden * gelu_slope).astype(jnp.bfloat16)
    grad_in = contract_first(tokens, grad_pre).astype(jnp.bfloat16)
    grad_out = contract_first(hidden, cotangent).astype(jnp.bfloat16)
    grad_tokens = contract_last(grad_pre, weight_in).astype(jnp.bfloat16)
    return (mixed, grad_tokens, grad_in, grad_out)
```

```python
import functools

import jax
import jax.numpy as jnp
from jax import lax
from jax.experimental import pallas as pl
from jax.experimental.pallas import tpu as pltpu
from jax.sharding import PartitionSpec as P

BF = jnp.bfloat16
F32 = jnp.float32
MB = 2**20
CORES = 2
VM = pl.BlockSpec(memory_space=pltpu.VMEM)
ANY = pl.BlockSpec(memory_space=pl.ANY)


def gelu_parts(pre_act):
    normal_cdf = 0.5 * (1.0 + jax.scipy.special.erf(pre_act * 0.7071067811865476))
    density = jnp.exp(-0.5 * pre_act * pre_act) * 0.3989422804014327
    return (pre_act * normal_cdf, normal_cdf + pre_act * density)


def contract_first(left_side, right_side):
    return lax.dot_general(
        left_side, right_side, (((0,), (0,)), ((), ())), preferred_element_type=F32
    )


def contract_last(left_side, right_side):
    return lax.dot_general(
        left_side, right_side, (((1,), (1,)), ((), ())), preferred_element_type=F32
    )


def in_hbm(array):
    return pltpu.with_memory_space_constraint(array, pltpu.HBM)


def chunk_of(size, limit):
    best = 128
    for width in range(128, min(size, limit) + 1, 128):
        if size % width == 0:
            best = width
    return best


def in_vmem(array):
    return pltpu.with_memory_space_constraint(array, pltpu.VMEM)


def call(kernel, args, outs, flops=0, moved=0, limit=6 * MB, scratch=(), aliases=None):
    return pl.pallas_call(
        kernel,
        in_specs=[spec for _, spec in args],
        out_specs=[spec for _, _, spec in outs],
        out_shape=[jax.ShapeDtypeStruct(shape, dtype) for shape, dtype, _ in outs],
        scratch_shapes=list(scratch),
        input_output_aliases=aliases or {},
        compiler_params=pltpu.CompilerParams(vmem_limit_bytes=limit),
        cost_estimate=pl.CostEstimate(flops=flops, bytes_accessed=moved, transcendentals=0),
    )(*[in_hbm(array) if spec is ANY else array for array, spec in args])


def load_kernel(tok, cot, out, tok_v, cot_v, sems):
    copies = [
        pltpu.make_async_copy(tok, tok_v, sems.at[0]),
        pltpu.make_async_copy(cot, cot_v, sems.at[1]),
    ]
    for copy in copies:
        copy.start()
    for copy in copies:
        copy.wait()
    both = [tok_v[...].astype(F32), cot_v[...].astype(F32)]
    out[...] = jnp.concatenate(both, axis=0).astype(BF)


def pack_kernel(after, *refs):
    ins, out = refs[:-1], refs[-1]
    rows = ins[0].shape[0] // 2
    blocks = [ref[...].astype(F32) for ref in ins]
    both = [block[:rows] for block in blocks] + [block[rows:] for block in blocks]
    out[...] = jnp.concatenate(both, axis=0).astype(BF)


def join_rows(mine, other, first, count):
    return jnp.concatenate([mine[first : first + count, :], other[first : first + count, :]], axis=0)


def tok_rows(mine, other):
    half = mine.shape[0] // 2
    return join_rows(mine, other, 0, half)


def cot_rows(mine, other):
    half = mine.shape[0] // 2
    return join_rows(mine, other, half, half)


def block_start(step, block):
    return pl.multiple_of((lax.axis_index("row") ^ step) * block, 128)


def stage_kernel(after, weight, held, sems):
    high = weight.shape[0] // sems.shape[0]
    copies = []
    for j in range(sems.shape[0]):
        at = pl.ds(j * high, high)
        copies.append(pltpu.make_async_copy(weight.at[at, :], held.at[at, :], sems.at[j]))
    for copy in copies:
        copy.start()
    for copy in copies:
        copy.wait()


def forward_kernel(mine, other, weight, *outs):
    block = outs[0].shape[1]
    width = chunk_of(block, 256)
    x = tok_rows(mine, other)
    for step, out in enumerate(outs):
        start = block_start(step, block)

        @pl.loop(0, block // width)
        def _(j):
            at = pl.multiple_of(j * width, 128)
            w = weight[:, pl.ds(pl.multiple_of(start + at, 128), width)]
            part = jnp.dot(x, w, preferred_element_type=F32)
            out[:, pl.ds(at, width)] = part.astype(out.dtype)


def backward_kernel(step, mine, other, pre, weight, out):
    rows, block = pre.shape
    w = weight[pl.ds(block_start(step, block), block), :]
    part = contract_last(w, cot_rows(mine, other)).T.astype(out.dtype)
    if step == 0:
        out[...] = part
    else:
        out[:rows, :] = pre[...]
        out[rows:, :] = part


def gelu_kernel(pre_own, grad_own, *refs):
    parts, out = refs[:-1], refs[-1]
    rows = pre_own.shape[0]
    pre, grad = pre_own[...], grad_own[...]
    for part in parts:
        pre = pre + part[:rows, :].astype(F32)
        grad = grad + part[rows:, :].astype(F32)
    value, slope = gelu_parts(pre)
    out[:rows, :] = value.astype(BF)
    out[rows:, :] = (grad * slope).astype(BF)


def add_up(n, pieces, w_in, w_out, keep, away, hidden, grad, held, sems):
    rows, block = hidden.shape[0], pieces[0].shape[1]
    half = rows // 2
    ring, high = held.shape[0], held.shape[1]
    count = w_in.shape[0] // high

    def copy(j):
        at = pl.ds(pl.multiple_of(j * high, 128), high)
        slot = lax.rem(j, ring)
        return pltpu.make_async_copy(w_in.at[at, :], held.at[slot], sems.at[slot])

    def begin():
        for j in range(ring):
            copy(jnp.int32(j)).start()

    def forward():
        for step, piece in enumerate(pieces):
            columns = pl.ds(block_start(step, block), block)
            hidden[:, columns] = piece[:rows, :]
            grad[:, columns] = piece[rows:, :]
        cols = w_out.shape[1]
        width = chunk_of(cols, 256)

        @pl.loop(0, cols // width)
        def _(j):
            columns = pl.ds(pl.multiple_of(j * width, 128), width)
            part = jnp.dot(hidden[...], w_out[:, columns], preferred_element_type=F32)
            keep[:half, columns] = part[:half]
            away[:half, columns] = part[half:]

    def backward():
        @pl.loop(0, count)
        def _(j):
            copy(j).wait()
            columns = pl.ds(pl.multiple_of(j * high, 128), high)
            part = contract_last(held[lax.rem(j, ring)], grad[...]).T
            keep[half:, columns] = part[:half]
            away[half:, columns] = part[half:]

            @pl.when(j + ring < count)
            def _():
                copy(j + ring).start()

    return begin, forward, backward


def write_grads(step, piece, tok_t, mine, other, grad_in, grad_out, in_v, out_v, in_sems, out_sems):
    rows, block = piece.shape[0] // 2, piece.shape[1]
    start = block_start(step, block)
    cot = cot_rows(mine, other)
    grad = piece[rows:, :]
    n_out, n_in = out_sems.shape[0], in_sems.shape[0]
    chunk, high = out_v.shape[0] // n_out, in_v.shape[0] // n_in

    def out_copy(j):
        at = pl.multiple_of(j * chunk, 128)
        to = pl.multiple_of(start + at, 128)
        return pltpu.make_async_copy(
            out_v.at[pl.ds(at, chunk), :], grad_out.at[pl.ds(to, chunk), :], out_sems.at[j]
        )

    def in_copy(j):
        at = pl.ds(pl.multiple_of(j * high, 128), high)
        return pltpu.make_async_copy(
            in_v.at[at, :], grad_in.at[at, pl.ds(start, block)], in_sems.at[j]
        )

    def product(left, right, place, first):
        tall, wide = chunk_of(left.shape[0], 256), chunk_of(right.shape[1], 256)
        for c in range(right.shape[1] // wide):
            columns = slice(c * wide, (c + 1) * wide)
            for r in range(left.shape[0] // tall):
                part = jnp.dot(
                    left[r * tall : (r + 1) * tall], right[:, columns], preferred_element_type=F32
                )
                at = pl.ds(pl.multiple_of(first + r * tall, 128), tall)
                place[at, columns] = part.astype(BF)

    @pl.loop(0, n_out)
    def _(j):
        first = pl.multiple_of(j * chunk, 128)
        left = piece[:rows, pl.ds(first, chunk)].astype(F32).T.astype(BF)
        product(left, cot, out_v, first)
        out_copy(j).start()

    @pl.loop(0, n_in)
    def _(j):
        first = pl.multiple_of(j * high, 128)
        product(tok_t[pl.ds(first, high), :], grad, in_v, first)
        in_copy(j).start()

    def finish():
        for j in range(n_out):
            out_copy(j).wait()
        for j in range(n_in):
            in_copy(j).wait()

    return finish


def first_kernel(piece, mine, other, _, tok_t, grad_in, grad_out, *scratch):
    tok_t[...] = tok_rows(mine, other).astype(F32).T.astype(BF)
    write_grads(0, piece, tok_t, mine, other, grad_in, grad_out, *[ref.at[0] for ref in scratch])()


def main_kernel(n, steps, *refs):
    pieces = refs[:n]
    mine, other, tok_t, w_in, w_out, _, _, keep, away, grad_in, grad_out = refs[n : n + 11]
    hidden, grad, held, sems = refs[n + 11 : n + 15]
    scratch = refs[n + 15 :]
    begin, forward, backward = add_up(n, pieces, w_in, w_out, keep, away, hidden, grad, held, sems)
    begin()
    for i, step in enumerate(steps):
        own = [ref.at[0] for ref in scratch]
        finish = write_grads(step, pieces[step], tok_t, mine, other, grad_in, grad_out, *own)
        if i == 0:
            forward()
        if i == len(steps) - 1:
            backward()
        finish()


def grads_kernel(steps, *refs):
    pieces = refs[: len(steps)]
    mine, other, tok_t, _, _, grad_in, grad_out = refs[len(steps) : len(steps) + 7]
    scratch = refs[len(steps) + 7 :]
    finish = []
    for i, step in enumerate(steps):
        own = [ref.at[i] for ref in scratch]
        finish.append(write_grads(step, pieces[i], tok_t, mine, other, grad_in, grad_out, *own))
    for end in finish:
        end()


def pair_kernel(keep, away, own, *outs):
    rows = own.shape[0] // 2
    half = keep.shape[0] // 2
    total = keep[...] + away[...]
    for k, out in enumerate((own,) + outs):
        out[:rows, :] = total[k * rows : (k + 1) * rows].astype(out.dtype)
        out[rows:, :] = total[half + k * rows : half + (k + 1) * rows].astype(out.dtype)


def final_kernel(*refs):
    parts, (mixed, back) = refs[:-2], refs[-2:]
    rows = mixed.shape[0]
    total = parts[0][...]
    for part in parts[1:]:
        total = total + part[...].astype(F32)
    mixed[...] = total[:rows].astype(BF)
    back[...] = total[rows:].astype(BF)


def split_plan(tokens, cotangent, weight_in, weight_out):
    n = lax.axis_size("row")
    n_col = lax.axis_size("col")
    z = n_col // CORES
    mine_rows, width = tokens.shape
    units = weight_in.shape[1]
    block = units // n
    rows = mine_rows * n_col
    flops = 2 * rows * width * units

    def along(array, k):
        pairs = []
        for c in range(CORES):
            for at in range(z):
                pairs.append((at * CORES + c, ((at + k) % z) * CORES + c))
        return lax.ppermute(array, "col", pairs)

    def swap(array):
        return lax.ppermute(array, "col", [(i, i ^ 1) for i in range(n_col)])

    def across(array, step):
        return lax.ppermute(array, "row", [(i, i ^ step) for i in range(n)])

    (packed,) = call(
        load_kernel,
        [(tokens, ANY), (cotangent, ANY)],
        [((2 * mine_rows, width), BF, VM)],
        scratch=[pltpu.VMEM((mine_rows, width), BF)] * 2 + [pltpu.SemaphoreType.DMA((2,))],
    )
    others = [along(packed, z - k) for k in range(1, z)]
    (held,) = call(
        stage_kernel,
        [(packed, VM), (weight_in, ANY)],
        [(weight_in.shape, BF, VM)],
        moved=2 * width * units,
        scratch=[pltpu.SemaphoreType.DMA((4,))],
        limit=2 * MB,
    )
    weights = [(in_vmem(held), VM), (in_vmem(weight_out), VM)]
    (mine,) = call(
        pack_kernel,
        [weights[0]] + [(a, VM) for a in [packed] + others],
        [((rows, width), BF, VM)],
    )
    common = [(mine, VM), (swap(mine), VM)]

    pres = call(
        forward_kernel,
        common + weights[:1],
        [((rows, block), F32, VM)] + [((rows, block), BF, VM)] * (n - 1),
        flops=flops,
        moved=2 * width * units,
    )

    def backward(step):
        shape = ((rows, block), F32, VM) if step == 0 else ((2 * rows, block), BF, VM)
        return call(
            functools.partial(backward_kernel, step),
            common + [(pres[step], VM), weights[1]],
            [shape],
            flops=flops // n,
            moved=2 * width * block,
        )[0]

    arrived = [(across(backward(step), step), VM) for step in range(n - 1, 0, -1)]
    own = [pres[0], backward(0)]
    (piece,) = call(
        gelu_kernel, [(a, VM) for a in own] + arrived, [((2 * rows, block), BF, VM)]
    )
    pieces = [piece] + [across(piece, step) for step in range(1, n)]

    grads = [((width, units), BF, ANY), ((units, width), BF, ANY)]
    n_in = width // chunk_of(width, 768)
    n_out = block // chunk_of(block, 256)

    def staging(count):
        return [
            pltpu.VMEM((count, width, block), BF),
            pltpu.VMEM((count, block, width), BF),
            pltpu.SemaphoreType.DMA((count, n_in)),
            pltpu.SemaphoreType.DMA((count, n_out)),
        ]

    tok_t, grad_in, grad_out = call(
        first_kernel,
        [(piece, VM)] + common + [weights[1]],
        [((width, rows), BF, VM)] + grads,
        flops=2 * flops // n,
        moved=4 * width * block,
        scratch=staging(1),
        limit=4 * width * block + 4 * MB,
    )

    inner = list(range(1, n - 1))
    high = chunk_of(width, 768)
    ring = min(2, width // high)
    keep, away, grad_in, grad_out = call(
        functools.partial(main_kernel, n, inner),
        [(a, VM) for a in pieces] + common + [(tok_t, VM), (weight_in, ANY), weights[1]]
        + [(grad_in, ANY), (grad_out, ANY)],
        [((rows, width), F32, VM)] * 2 + grads,
        flops=2 * flops + 2 * len(inner) * flops // n,
        moved=4 * width * units + 4 * len(inner) * width * block,
        scratch=[pltpu.VMEM((rows, units), BF)] * 2
        + [pltpu.VMEM((ring, high, units), BF), pltpu.SemaphoreType.DMA((ring,))]
        + staging(1),
        limit=2 * ring * high * units + 4 * width * block + 5 * MB,
        aliases={n + 5: 2, n + 6: 3},
    )
    away = swap(away)
    totals = call(
        pair_kernel,
        [(keep, VM), (away, VM)],
        [((2 * mine_rows, width), F32, VM)] + [((2 * mine_rows, width), BF, VM)] * (z - 1),
    )
    parts = [totals[0]] + [along(totals[k], k) for k in range(1, z)]
    last = [n - 1]
    grad_in, grad_out = call(
        functools.partial(grads_kernel, last),
        [(pieces[step], VM) for step in last] + common
        + [(tok_t, VM), (grad_in, ANY), (grad_out, ANY)],
        grads,
        flops=2 * flops // n,
        moved=4 * width * block,
        scratch=staging(1),
        limit=4 * width * block + 4 * MB,
        aliases={4: 0, 5: 1},
    )
    mixed, grad_tokens = call(
        final_kernel, [(a, VM) for a in parts], [((mine_rows, width), BF, VM)] * 2
    )
    return (mixed, grad_tokens, grad_in, grad_out)


def plain_plan(tokens, cotangent, weight_in, weight_out):
    tok_all = lax.all_gather(tokens, "col", axis=0, tiled=True)
    cot_all = lax.all_gather(cotangent, "col", axis=0, tiled=True)
    pre = lax.psum_scatter(
        jnp.dot(tok_all, weight_in, preferred_element_type=F32),
        "row", scatter_dimension=0, tiled=True,
    )
    value, slope = gelu_parts(pre)
    hidden = lax.all_gather(value.astype(BF), "row", axis=0, tiled=True)
    grad_hidden = lax.psum_scatter(
        contract_last(cot_all, weight_out), "row", scatter_dimension=0, tiled=True
    )
    grad_pre = lax.all_gather((grad_hidden * slope).astype(BF), "row", axis=0, tiled=True)
    mixed = lax.psum_scatter(
        jnp.dot(hidden, weight_out, preferred_element_type=F32),
        "col", scatter_dimension=0, tiled=True,
    ).astype(BF)
    grad_tokens = lax.psum_scatter(
        contract_last(grad_pre, weight_in), "col", scatter_dimension=0, tiled=True
    ).astype(BF)
    grad_in = contract_first(tok_all, grad_pre).astype(BF)
    grad_out = contract_first(hidden, cot_all).astype(BF)
    return (mixed, grad_tokens, grad_in, grad_out)


def shards(tokens, cotangent, weight_in, weight_out):
    n, n_col = lax.axis_size("row"), lax.axis_size("col")
    fits = (
        n >= 4
        and n & (n - 1) == 0
        and n_col % CORES == 0
        and tokens.shape[0] % 8 == 0
        and weight_in.shape[0] % 128 == 0
        and weight_in.shape[1] % (128 * n) == 0
        and (tokens.shape[0] * n_col) % 64 == 0
    )
    plan = split_plan if fits else plain_plan
    return plan(tokens, cotangent, weight_in, weight_out)


def solution(mesh):
    return jax.shard_map(
        shards,
        mesh=mesh,
        in_specs=(P("col", "row"), P("col", "row"), P("row", "col"), P("col", "row")),
        out_specs=(P("col", "row"), P("col", "row"), P("row", "col"), P("col", "row")),
        check_vma=False,
    )
```
